128 devices in a mesh: group: 4 (over z), shard: 32 (over y, x, core).
Axes of the slice: x: 4, y: 4, z: 4, core: 2. Of those that a mesh axis runs over, the one named last changes fastest.
Arguments:
- item_factors: float32 [131072, 256], P(('group', 'shard')), may hold values from -0.015625 to 0.015625
- item_block: int32 [128, 128], P(('group', 'shard')), may hold values from 0 to 1023, as said below
- tile_user: int32 [128, 128], P(('group', 'shard')), may hold values from 0 to 3, as said below
- tile_count: int32 [128], P(('group', 'shard')), may hold values from 96 to 128, as said below
- tile_counts: int32 [16384, 128, 128], P(('group', 'shard')), may hold values from 1 to 8
Outputs:
- user_factors: float32 [65536, 256], P('shard')
The draws below stay inside these ranges and needn't reach their ends.
Inputs may be any that keep to these rules, and one draw needn't show every extreme that they name: In every row, at most 2 slots name item blocks with one value of item_block // 8; the first two slots of every row name the same such value. `tile_user`: the first 4 slots of every row name every user block once. `tile_count`: some row has 128 live slots.
All inputs are finite; a program needn't handle non-finite values.
Results may differ from the reference program's by a relative error of at most 0.0003.
Values sent between devices are 32-bit elements; how exact they have to be, the bound alone decides.
A program may use at most 192 MiB of HBM per device.

```python
import jax
import jax.numpy as jnp
from jax import lax

FEAT = 256
TILE = 128
UB_DEV = 4
IB_DEV = 8
SLOTS = 2
CG_ITERS = 3
TILE_MAX = 128
ITEMS = 131072
USERS = 65536
N_GROUP = 4
N_SHARD = 32
DEVICES = 128


def draw_item_block(key, part):
    key = jax.random.fold_in(key, 11)

    def one_row(row_key):
        first_key, second_key = jax.random.split(row_key, 2)
        owners_all = jnp.arange(SLOTS * DEVICES, dtype=jnp.int32) // SLOTS
        sequence = owners_all[jax.random.permutation(first_key, SLOTS * DEVICES)]
        leader = sequence[0]
        partner = 1 + jnp.argmax((sequence[1:] == leader).astype(jnp.int32))
        displaced = sequence[1]
        sequence = sequence.at[partner].set(displaced).at[1].set(leader)
        owners = sequence[:TILE_MAX]
        local_slot = jax.random.randint(second_key, (TILE_MAX,), 0, IB_DEV, dtype=jnp.int32)
        return owners * IB_DEV + local_slot
    return jax.vmap(one_row)(jax.random.split(key, DEVICES)).astype(jnp.int32)


def draw_tile_user(key, part):
    key = jax.random.fold_in(key, 23)
    first_key, second_key = jax.random.split(key, 2)
    random_users = jax.random.randint(first_key, (DEVICES, TILE_MAX), 0, UB_DEV, dtype=jnp.int32)

    def one_perm(row_key):
        return jax.random.permutation(row_key, jnp.arange(UB_DEV, dtype=jnp.int32))
    leading = jax.vmap(one_perm)(jax.random.split(second_key, DEVICES))
    return random_users.at[:, :UB_DEV].set(leading).astype(jnp.int32)


def draw_tile_count(key, part):
    key = jax.random.fold_in(key, 37)
    first_key, third_key = jax.random.split(key, 2)
    lowest = 3 * TILE_MAX // 4
    counts = jax.random.randint(first_key, (DEVICES,), lowest, TILE_MAX + 1, dtype=jnp.int32)
    busiest = jax.random.randint(third_key, (), 0, DEVICES, dtype=jnp.int32)
    return counts.at[busiest].set(TILE_MAX).astype(jnp.int32)


def set_ends(values, rng, low, high):
    index_at = [jax.random.randint(jax.random.fold_in(rng, axis), (), 0, length) for axis, length in enumerate(values.shape)]
    widest = values.shape.index(max(values.shape))
    neighbour = index_at[:widest] + [(index_at[widest] + 1) % values.shape[widest]] + index_at[widest + 1:]
    return values.at[tuple(index_at)].set(low).at[tuple(neighbour)].set(high)


def shard_levels(rng, dims, pieces, low, high):
    loudness = 1.0
    for axis_at, blocks in pieces:
        heights = jax.random.uniform(jax.random.fold_in(jax.random.fold_in(rng, 6), axis_at), (blocks,), jnp.float32, low / len(pieces), high / len(pieces))
        loudness = loudness * jnp.repeat(jnp.exp(heights), dims[axis_at] // blocks).reshape((-1,) + (1,) * (len(dims) - 1 - axis_at))
    return loudness


def scatter_about(stream_key, extent, spread, bound, pieces=(), kind=jnp.bfloat16):
    array = spread * jax.random.normal(stream_key, extent, jnp.float32)
    if pieces:
        array = array * shard_levels(stream_key, extent, pieces, -0.22, 0.18)
    return jnp.clip(array, -bound, bound).astype(kind)


def setup_inputs(seed: int = 0) -> dict:
    arg_keys = jax.random.split(jax.random.key(seed), 6)
    item_factors = scatter_about(arg_keys[0], (ITEMS, FEAT), ITEMS ** -0.5, 0.015625, ((0, 128),), jnp.float32)
    item_block = draw_item_block(jax.random.fold_in(arg_keys[5], 71), 0)
    tile_user = draw_tile_user(jax.random.fold_in(arg_keys[5], 71), 0)
    tile_count = draw_tile_count(jax.random.fold_in(arg_keys[5], 71), 0)
    tile_counts = set_ends(jax.random.randint(arg_keys[4], (DEVICES * TILE_MAX, TILE, TILE), 1, 9), jax.random.fold_in(arg_keys[4], 1), 1, 8).astype(jnp.int32)
    return dict(item_factors=item_factors, item_block=item_block, tile_user=tile_user, tile_count=tile_count, tile_counts=tile_counts)


confidence_scale = 8.0
ridge_weight = 0.1
highest = lax.Precision.HIGHEST


def reference(item_factors, item_block, tile_user, tile_count, tile_counts):
    gram = jnp.dot(item_factors.T, item_factors, precision=highest, preferred_element_type=jnp.float32)
    blocks = item_factors.reshape(-1, TILE, FEAT)
    counts = tile_counts.reshape(DEVICES, TILE_MAX, TILE, TILE)

    def solve_row(packed):
        blocks_row, users_row, live_count, counts_row = packed
        item_rows = jnp.take(blocks, blocks_row, axis=0)
        weights = counts_row.astype(jnp.float32)
        live = jnp.arange(TILE_MAX) < live_count
        chooser = ((users_row[None, :] == jnp.arange(UB_DEV)[:, None]) & live[None, :]).astype(jnp.float32)

        def block_sum(terms):
            return jnp.einsum('bt,tuf->buf', chooser, terms, precision=highest)

        right = block_sum(jnp.einsum('tui,tif->tuf', 1.0 + confidence_scale * weights, item_rows, precision=highest))

        def operate(direction):
            taken = jnp.take(direction, users_row, axis=0)
            scores = jnp.einsum('tuf,tif->tui', taken, item_rows, precision=highest) * (confidence_scale * weights)
            tiles = jnp.einsum('tui,tif->tuf', scores, item_rows, precision=highest)
            dense = jnp.einsum('buf,fg->bug', direction, gram, precision=highest)
            return dense + ridge_weight * direction + block_sum(tiles)

        solution = jnp.zeros_like(right)
        residual = right
        direction = right
        norm_now = jnp.sum(residual * residual, axis=-1, keepdims=True)
        for iteration in range(CG_ITERS):
            image = operate(direction)
            step_size = norm_now / jnp.sum(direction * image, axis=-1, keepdims=True)
            solution = solution + step_size * direction
            residual = residual - step_size * image
            norm_next = jnp.sum(residual * residual, axis=-1, keepdims=True)
            direction = residual + (norm_next / norm_now) * direction
            norm_now = norm_next
        return solution

    solved = lax.map(solve_row, (item_block, tile_user, tile_count, counts))
    solved = solved.reshape(N_GROUP, N_SHARD, UB_DEV * TILE, FEAT)
    return jnp.transpose(solved, (1, 0, 2, 3)).reshape(USERS, FEAT)
```

```python
import functools

import jax
import jax.numpy as jnp
from jax import lax
from jax.experimental import pallas as pl
from jax.experimental.pallas import tpu as pltpu
from jax.sharding import PartitionSpec as P

UB_DEV = 4
IB_DEV = 8
CG_ITERS = 3
TILE = 128
FEAT = 256
CONFIDENCE = 8.0
RIDGE = 0.1
MESH = pl.DeviceIdType.MESH

PART_ROWS = (48, 40, 40)
PART_FIRST = (0, 48, 88)
ROUTES = (("x", "y", "z"), ("y", "z", "x"), ("z", "x", "y"))
PARTS = 3
SIDE = 4
CORES = 2
HALF = IB_DEV // 2
PLANE = SIDE * SIDE * IB_DEV
CHUNK = 4
BUFFERS = 4
USUAL = 40
MOST = 64


def route_of(p, core):
    return ROUTES[(p + core) % PARTS]


def my_coords():
    shard = lax.axis_index("shard")
    return {
        "z": lax.axis_index("group"),
        "y": shard // (SIDE * CORES),
        "x": (shard // CORES) % SIDE,
        "core": shard % CORES,
    }


def device_at(coords):
    return (coords["z"], (coords["y"] * SIDE + coords["x"]) * CORES + coords["core"])


def shifted(coords, axis, offset):
    moved = dict(coords)
    moved[axis] = (coords[axis] + offset) % (CORES if axis == "core" else SIDE)
    return moved


def place(coords, p, turn):
    core = coords["core"]
    return coords[route_of(p, 0)[turn]] * (1 - core) + coords[route_of(p, 1)[turn]] * core


def along(coords, p, turn, offset):
    core = coords["core"]
    moved = dict(coords)
    for axis, here in ((route_of(p, 0)[turn], 1 - core), (route_of(p, 1)[turn], core)):
        moved[axis] = (coords[axis] + offset * here) % SIDE
    return device_at(moved)


def exchange_kernel(cap, piece, items_ref, lists_ref, r0_ref, r1_ref, r2_ref, p0_ref, p1_ref, p2_ref,
                    s0_ref, s1_ref, s2_ref, asked_ref, asked_smem, own_sem, smem_sem, list_send, list_recv,
                    first_send, first_recv, second_send, second_recv, third_send, third_recv, side_send,
                    side_recv, keep_sem):
    received = (r0_ref, r1_ref, r2_ref)
    planes = (p0_ref, p1_ref, p2_ref)
    staged = (s0_ref, s1_ref, s2_ref)
    pieces = cap // piece
    me = my_coords()
    sibling = device_at(shifted(me, "core", 1))

    barrier = pltpu.get_barrier_semaphore()
    for axis in ("x", "y", "z"):
        for offset in (1, 2, 3):
            pl.semaphore_signal(barrier, inc=1, device_id=device_at(shifted(me, axis, offset)), device_id_type=MESH)
    pl.semaphore_signal(barrier, inc=1, device_id=sibling, device_id_type=MESH)

    loads = []
    for p in range(PARTS):
        own = (place(me, p, 1) * SIDE + place(me, p, 0)) * IB_DEV
        loads.append(
            pltpu.make_async_copy(
                items_ref.at[:, pl.ds(PART_FIRST[p], PART_ROWS[p]), :],
                planes[p].at[pl.ds(own, IB_DEV)],
                own_sem.at[p],
            )
        )
        loads[p].start()
    pl.semaphore_wait(barrier, 10)

    list_copies = []
    for p in range(PARTS):
        for offset in (1, 2, 3):
            slot = SIDE - offset
            copy = pltpu.make_async_remote_copy(
                src_ref=lists_ref.at[p, (place(me, p, 2) + offset) % SIDE],
                dst_ref=asked_ref.at[p, slot],
                send_sem=list_send.at[p, slot],
                recv_sem=list_recv.at[p, slot],
                device_id=along(me, p, 2, offset),
                device_id_type=MESH,
            )
            copy.start()
            list_copies.append(copy)

    def plane_copy(p, db, da, half, turn, offset, send_sem, recv_sem):
        at = (((place(me, p, 1) + db) % SIDE) * SIDE + (place(me, p, 0) + da) % SIDE) * IB_DEV
        if half is None:
            where = pl.ds(at, IB_DEV)
        else:
            where = pl.ds(at + half * HALF, HALF)
        return pltpu.make_async_remote_copy(
            src_ref=planes[p].at[where],
            dst_ref=planes[p].at[where],
            send_sem=send_sem,
            recv_sem=recv_sem,
            device_id=along(me, p, turn, offset),
            device_id_type=MESH,
        )

    def first(p, slot):
        da, half, offset = ((0, None, 1), (0, None, 3), (3, 0, 1), (1, 1, 3))[slot]
        return plane_copy(p, 0, da, half, 0, offset, first_send.at[p, slot], first_recv.at[p, slot])

    def second(p, da, slot):
        db, half, offset = ((0, None, 1), (0, None, 3), (3, 0, 1), (1, 1, 3))[slot]
        return plane_copy(
            p, db, da, half, 1, offset, second_send.at[p, da, slot], second_recv.at[p, da, slot]
        )

    for p in range(PARTS):
        loads[p].wait()
        first(p, 0).start()
        first(p, 1).start()
        second(p, 0, 0).start()
        second(p, 0, 1).start()
    for p in range(PARTS):
        first(p, 0).wait_recv()
        first(p, 2).start()
        second(p, 3, 0).start()
        second(p, 3, 1).start()
        first(p, 1).wait_recv()
        first(p, 3).start()
        second(p, 1, 0).start()
        second(p, 1, 1).start()
    for p in range(PARTS):
        second(p, 0, 0).wait_recv()
        second(p, 0, 2).start()
        second(p, 0, 1).wait_recv()
        second(p, 0, 3).start()
    for p in range(PARTS):
        first(p, 2).wait_recv()
        first(p, 3).wait_recv()
        second(p, 2, 0).start()
        second(p, 2, 1).start()
    for da in (3, 1, 2):
        for p in range(PARTS):
            second(p, da, 0).wait_recv()
            second(p, da, 2).start()
            second(p, da, 1).wait_recv()
            second(p, da, 3).start()

    for copy in list_copies:
        copy.wait()
    for p in range(PARTS):
        for offset in range(SIDE):
            source = lists_ref.at[p, place(me, p, 2)] if offset == 0 else asked_ref.at[p, offset]
            copy = pltpu.make_async_copy(source, asked_smem.at[p, offset], smem_sem.at[p, offset])
            copy.start()
    for p in range(PARTS):
        for offset in range(SIDE):
            pltpu.make_async_copy(lists_ref.at[p, 0], asked_smem.at[p, offset], smem_sem.at[p, offset]).wait()
    for da in (0, 3, 1, 2):
        for p in range(PARTS):
            second(p, da, 2).wait_recv()
            second(p, da, 3).wait_recv()

    def slots_of(p, offset, core, start):
        at = ((place(me, p, 2) + offset) % SIDE * CORES + core) * MOST
        return pl.ds(at + start, piece)

    def third(p, offset, i):
        return pltpu.make_async_remote_copy(
            src_ref=staged[p].at[offset, pl.ds(i * piece, piece)],
            dst_ref=received[p].at[slots_of(p, 0, me["core"], i * piece)],
            send_sem=third_send.at[p, SIDE - offset, i],
            recv_sem=third_recv.at[p, SIDE - offset, i],
            device_id=along(me, p, 2, offset),
            device_id_type=MESH,
        )

    def side(p, offset, i):
        here = received[p].at[slots_of(p, offset, me["core"], i * piece)]
        source = staged[p].at[0, pl.ds(i * piece, piece)] if offset == 0 else here
        return pltpu.make_async_remote_copy(
            src_ref=source,
            dst_ref=here,
            send_sem=side_send.at[p, offset, i],
            recv_sem=side_recv.at[p, offset, i],
            device_id=sibling,
            device_id_type=MESH,
        )

    def keep(p, i):
        return pltpu.make_async_copy(
            staged[p].at[0, pl.ds(i * piece, piece)],
            received[p].at[slots_of(p, 0, me["core"], i * piece)],
            keep_sem.at[p, i],
        )

    def stage(p, offset, i):
        def one(j, carry):
            at = i * piece + j
            staged[p][offset, at] = planes[p][asked_smem[p, offset, 0, at]]
            return carry

        lax.fori_loop(0, piece, one, 0)

    def send_pieces(i, carry):
        for p in range(PARTS):
            for offset in (2, 1, 3):
                stage(p, offset, i)
                third(p, offset, i).start()
        return carry

    lax.fori_loop(0, pieces, send_pieces, 0)

    def keep_pieces(i, carry):
        for p in range(PARTS):
            stage(p, 0, i)
            keep(p, i).start()
            side(p, 0, i).start()
        return carry

    lax.fori_loop(0, pieces, keep_pieces, 0)

    def pass_pieces(i, carry):
        for p in range(PARTS):
            for offset in (1, 2, 3):
                third(p, SIDE - offset, i).wait_recv()
                side(p, offset, i).start()
        return carry

    lax.fori_loop(0, pieces, pass_pieces, 0)

    def end_pieces(i, carry):
        for p in range(PARTS):
            keep(p, i).wait()
            for offset in range(SIDE):
                side(p, offset, i).wait()
                if offset:
                    third(p, offset, i).wait_send()
        return carry

    lax.fori_loop(0, pieces, end_pieces, 0)
    for p in range(PARTS):
        for slot in range(4):
            first(p, slot).wait_send()
            for da in range(SIDE):
                second(p, da, slot).wait_send()


def exchange(items, lists, cap, piece, collective_id):
    pieces = cap // piece
    dma = pltpu.SemaphoreType.DMA
    return pl.pallas_call(
        functools.partial(exchange_kernel, cap, piece),
        out_shape=[
            jax.ShapeDtypeStruct((SIDE * CORES * MOST, rows, FEAT), jnp.float32) for rows in PART_ROWS
        ],
        in_specs=[pl.BlockSpec(memory_space=pl.ANY), pl.BlockSpec(memory_space=pltpu.VMEM)],
        out_specs=[pl.BlockSpec(memory_space=pl.ANY)] * PARTS,
        scratch_shapes=[pltpu.VMEM((PLANE, rows, FEAT), jnp.float32) for rows in PART_ROWS]
        + [pltpu.VMEM((SIDE, cap, rows, FEAT), jnp.float32) for rows in PART_ROWS]
        + [
            pltpu.VMEM((PARTS, SIDE, 8, TILE), jnp.int32),
            pltpu.SMEM((PARTS, SIDE, 8, TILE), jnp.int32),
            dma((PARTS,)),
            dma((PARTS, SIDE)),
            dma((PARTS, SIDE)),
            dma((PARTS, SIDE)),
            dma((PARTS, 4)),
            dma((PARTS, 4)),
            dma((PARTS, SIDE, 4)),
            dma((PARTS, SIDE, 4)),
            dma((PARTS, SIDE, pieces)),
            dma((PARTS, SIDE, pieces)),
            dma((PARTS, SIDE, pieces)),
            dma((PARTS, SIDE, pieces)),
            dma((PARTS, pieces)),
        ],
        compiler_params=pltpu.CompilerParams(
            collective_id=collective_id, has_side_effects=True, vmem_limit_bytes=60 << 20
        ),
        name=f"exchange_{cap}",
    )(items.reshape(IB_DEV, TILE, FEAT), lists)


def split(values):
    high = values.astype(jnp.bfloat16)
    return high, (values - high.astype(jnp.float32)).astype(jnp.bfloat16)


def dot(left, right):
    return lax.dot_general(left, right, (((1,), (0,)), ((), ())), preferred_element_type=jnp.float32)


def split_product(left, high, low):
    rows = left.shape[0]
    left_high, left_low = split(left)
    both = dot(jnp.concatenate([left_high, left_low], axis=0), high)
    return both[:rows] + both[rows:] + dot(left_high, low)


def solve_kernel(first, plan_ref, gram_ref, r0_ref, r1_ref, r2_ref, counts_ref,
                 out_ref, order, rows_buf, counts_buf, high_ref, low_ref, high_t_ref, low_t_ref, weight_ref, sems):
    received = (r0_ref, r1_ref, r2_ref)
    b = first + pl.program_id(0)

    def append(k, total):
        order[total] = k
        return total + (plan_ref[PARTS, k] == b).astype(jnp.int32)

    total = lax.fori_loop(0, TILE, append, 0, unroll=8)
    chunks = (total + CHUNK - 1) // CHUNK

    def copies(i, slot):
        result = []
        for t in range(CHUNK):
            k = order[jnp.minimum(i * CHUNK + t, total - 1)]
            for p in range(PARTS):
                result.append(
                    pltpu.make_async_copy(
                        received[p].at[plan_ref[p, k]],
                        rows_buf.at[slot, pl.ds(t * TILE + PART_FIRST[p], PART_ROWS[p])],
                        sems.at[slot, t, p],
                    )
                )
            result.append(pltpu.make_async_copy(counts_ref.at[k], counts_buf.at[slot, t], sems.at[slot, t, PARTS]))
        return result

    def fetch(i):
        @pl.when(i < chunks)
        def _():
            for copy in copies(i, lax.rem(i, BUFFERS)):
                copy.start()

    for i in range(BUFFERS - 1):
        fetch(i)

    def load(i, right):
        slot = lax.rem(i, BUFFERS)
        fetch(i + BUFFERS - 1)
        for copy in copies(i, slot):
            copy.wait()
        high, low = split(rows_buf[slot])
        high_ref[i] = high
        low_ref[i] = low
        high_t_ref[i] = high.T
        low_t_ref[i] = low.T
        ones = []
        for t in range(CHUNK):
            live = (i * CHUNK + t < total).astype(jnp.float32)
            weight = counts_buf[slot, t].astype(jnp.float32) * (CONFIDENCE * live)
            weight_ref[i, :, t * TILE:(t + 1) * TILE] = weight.astype(jnp.bfloat16)
            ones.append((weight + live).astype(jnp.bfloat16))
        ones = jnp.concatenate(ones, axis=1)
        return right + dot(ones, high) + dot(ones, low)

    right = lax.fori_loop(0, chunks, load, jnp.zeros((TILE, FEAT), jnp.float32))
    gram_high, gram_low = split(gram_ref[...])

    solved = jnp.zeros_like(right)
    residual = right
    direction = right
    norm_now = jnp.sum(residual * residual, axis=-1, keepdims=True)
    for iteration in range(CG_ITERS):
        base = split_product(direction, gram_high, gram_low) + RIDGE * direction
        if iteration < CG_ITERS - 1:

            def scaled(i):
                scores = split_product(direction, high_t_ref[i], low_t_ref[i])
                return split(scores * weight_ref[i].astype(jnp.float32))

            def image_of(halves, i):
                both = dot(jnp.concatenate(halves, axis=0), high_ref[i])
                return both[:TILE] + both[TILE:] + dot(halves[0], low_ref[i])

            def apply(i, carry):
                running, high, low = carry
                running = running + image_of((high, low), i - 1)
                return (running,) + scaled(i)

            image, last_high, last_low = lax.fori_loop(1, chunks, apply, (base,) + scaled(0))
            image = image + image_of((last_high, last_low), chunks - 1)
            curve = jnp.sum(direction * image, axis=-1, keepdims=True)
        else:
            direction_halves = jnp.concatenate(split(direction), axis=0)

            def energy(i, running):
                both = dot(direction_halves, high_t_ref[i])
                scores = both[:TILE] + both[TILE:]
                return running + jnp.sum(scores * scores * weight_ref[i].astype(jnp.float32), axis=-1, keepdims=True)

            curve = lax.fori_loop(0, chunks, energy, jnp.sum(direction * base, axis=-1, keepdims=True))
        step = norm_now / curve
        solved = solved + step * direction
        if iteration < CG_ITERS - 1:
            residual = residual - step * image
            norm_next = jnp.sum(residual * residual, axis=-1, keepdims=True)
            direction = residual + norm_next / norm_now * direction
            norm_now = norm_next
    out_ref[...] = solved


def solve(first, count, places, gram, received, counts):
    smem = pl.BlockSpec(memory_space=pltpu.SMEM)
    vmem = pl.BlockSpec(memory_space=pltpu.VMEM)
    hbm = pl.BlockSpec(memory_space=pl.ANY)
    most = TILE // CHUNK
    return pl.pallas_call(
        functools.partial(solve_kernel, first),
        grid=(count,),
        out_shape=jax.ShapeDtypeStruct((count * TILE, FEAT), jnp.float32),
        in_specs=[smem, vmem] + [hbm] * 4,
        out_specs=pl.BlockSpec((TILE, FEAT), lambda b: (b, 0)),
        scratch_shapes=[
            pltpu.SMEM((TILE,), jnp.int32),
            pltpu.VMEM((BUFFERS, CHUNK * TILE, FEAT), jnp.float32),
            pltpu.VMEM((BUFFERS, CHUNK, TILE, TILE), jnp.int32),
            pltpu.VMEM((most, CHUNK * TILE, FEAT), jnp.bfloat16),
            pltpu.VMEM((most, CHUNK * TILE, FEAT), jnp.bfloat16),
            pltpu.VMEM((most, FEAT, CHUNK * TILE), jnp.bfloat16),
            pltpu.VMEM((most, FEAT, CHUNK * TILE), jnp.bfloat16),
            pltpu.VMEM((most, TILE, CHUNK * TILE), jnp.bfloat16),
            pltpu.SemaphoreType.DMA((BUFFERS, CHUNK, PARTS + 1)),
        ],
        cost_estimate=pl.CostEstimate(flops=8_000_000_000, bytes_accessed=16 << 20, transcendentals=0),
        compiler_params=pltpu.CompilerParams(vmem_limit_bytes=56 << 20),
        name=f"solve_{first}",
    )(places, gram, *received, counts)


def share_kernel(mine_ref, out_ref, send, recv, keep):
    me = my_coords()
    barrier = pltpu.get_barrier_semaphore()
    for offset in (1, 2, 3):
        pl.semaphore_signal(barrier, inc=1, device_id=device_at(shifted(me, "z", offset)), device_id_type=MESH)
    own = pltpu.make_async_copy(mine_ref, out_ref.at[me["z"]], keep)
    own.start()
    pl.semaphore_wait(barrier, 3)
    remotes = [
        pltpu.make_async_remote_copy(
            src_ref=mine_ref,
            dst_ref=out_ref.at[me["z"]],
            send_sem=send.at[offset],
            recv_sem=recv.at[offset],
            device_id=device_at(shifted(me, "z", offset)),
            device_id_type=MESH,
        )
        for offset in (1, 2, 3)
    ]
    for copy in remotes:
        copy.start()
    own.wait()
    for copy in remotes:
        copy.wait()


def share(mine):
    return pl.pallas_call(
        share_kernel,
        out_shape=jax.ShapeDtypeStruct((SIDE,) + mine.shape, jnp.float32),
        in_specs=[pl.BlockSpec(memory_space=pltpu.VMEM)],
        out_specs=pl.BlockSpec(memory_space=pltpu.VMEM),
        scratch_shapes=[
            pltpu.SemaphoreType.DMA((SIDE,)),
            pltpu.SemaphoreType.DMA((SIDE,)),
            pltpu.SemaphoreType.DMA,
        ],
        compiler_params=pltpu.CompilerParams(collective_id=2, has_side_effects=True),
        name="share",
    )(mine)


def plan(blocks_row, users_row, live_count, core):
    slots = blocks_row.shape[0]
    shard_size = lax.axis_size("shard")
    asked = jnp.where(jnp.arange(slots) < live_count, blocks_row, -1)
    other = lax.ppermute(asked, "shard", [(s, s ^ 1) for s in range(shard_size)])
    both = jnp.concatenate([asked, other])
    block_total = SIDE * SIDE * SIDE * CORES * IB_DEV
    needed = jnp.any(both[:, None] == jnp.arange(block_total)[None, :], axis=0)
    needed = needed.astype(jnp.float32).reshape(SIDE, SIDE, SIDE, CORES, IB_DEV)
    axes = {"z": 0, "y": 1, "x": 2}
    turns = {(p, k): [axes[axis] for axis in route_of(p, k)] for p in range(PARTS) for k in range(CORES)}
    ordered = jnp.stack([
        jnp.stack([
            jnp.transpose(needed[:, :, :, k], turns[p, k][::-1] + [3]).reshape(SIDE, PLANE) for k in range(CORES)
        ])
        for p in range(PARTS)
    ])
    before = (jnp.arange(PLANE)[:, None] < jnp.arange(PLANE)[None, :]).astype(jnp.float32)
    rank = jnp.einsum("pksi,ij->pksj", ordered, before, preferred_element_type=jnp.float32).astype(jnp.int32)
    most = jnp.max(jnp.sum(ordered, axis=-1))
    mine = lax.dynamic_index_in_dim(ordered, core, 1, keepdims=False) > 0
    mine_rank = lax.dynamic_index_in_dim(rank, core, 1, keepdims=False)
    hits = jnp.logical_and(mine[:, :, None, :], mine_rank[:, :, None, :] == jnp.arange(TILE)[:, None])
    lists = jnp.sum(jnp.where(hits, jnp.arange(PLANE, dtype=jnp.int32), 0), axis=-1)
    lists = jnp.broadcast_to(lists[:, :, None, :], (PARTS, SIDE, 8, TILE))
    tables = []
    for p in range(PARTS):
        sides = []
        for k in range(CORES):
            back = [turns[p, k][::-1].index(axis) for axis in range(3)] + [3]
            sides.append(jnp.transpose(rank[p, k].reshape(SIDE, SIDE, SIDE, IB_DEV), back))
        tables.append(jnp.stack(sides, axis=3).reshape(block_total))
    ranks = jnp.stack(tables)
    block = jnp.arange(block_total)
    where = {"z": block // 256, "y": block // 64 % 4, "x": block // 16 % 4}
    source_core = block // IB_DEV % CORES
    source = jnp.stack([
        jnp.where(source_core == 0, where[route_of(p, 0)[2]], where[route_of(p, 1)[2]]) * CORES + source_core
        for p in range(PARTS)
    ])
    table = source * MOST + jnp.minimum(ranks, MOST - 1)
    picked = blocks_row[:, None] == block[None, :]
    places = jnp.sum(jnp.where(picked[None], table[:, None, :], 0), axis=-1)
    users = jnp.where(jnp.arange(slots) < live_count, users_row, UB_DEV)
    places = jnp.concatenate([places, users[None], jnp.zeros((8 - PARTS - 1, slots), jnp.int32)])
    return lists, places, most


def body(item_factors, item_block, tile_user, tile_count, tile_counts):
    blocks_row = item_block[0]
    users_row = tile_user[0]
    core = lax.axis_index("shard") % CORES
    lists, places, most = plan(blocks_row, users_row, tile_count[0], core)
    local_gram = jnp.dot(
        item_factors.T, item_factors, precision=lax.Precision.HIGHEST, preferred_element_type=jnp.float32
    )
    over = jnp.full((8, FEAT), (most > USUAL).astype(jnp.float32))
    total = lax.psum(jnp.concatenate([local_gram, over]), ("group", "shard"))
    gram = total[:FEAT]
    received = exchange(item_factors, lists, USUAL, 8, 0)
    again = total[FEAT, 0] > 0
    _, received = lax.while_loop(
        lambda carry: carry[0],
        lambda carry: (jnp.zeros_like(again), exchange(item_factors, lists, MOST, 16, 1)),
        (again, received),
    )
    half = UB_DEV // 2
    earlier = solve(0, half, places, gram, received, tile_counts)
    earlier = lax.all_gather(earlier, "group", axis=0)
    later = solve(half, half, places, gram, received, tile_counts)
    return jnp.concatenate([earlier, share(later)], axis=1).reshape(-1, FEAT)


def solution(mesh):
    return jax.shard_map(
        body,
        mesh=mesh,
        in_specs=(
            P(("group", "shard"), None),
            P(("group", "shard"), None),
            P(("group", "shard"), None),
            P(("group", "shard")),
            P(("group", "shard"), None, None),
        ),
        out_specs=P("shard", None),
        check_vma=False,
    )
```

```python
import functools

import jax
import jax.numpy as jnp
from jax import lax
from jax.experimental import pallas as pl
from jax.experimental.pallas import tpu as pltpu
from jax.sharding import PartitionSpec as P

UB_DEV = 4
IB_DEV = 8
CG_ITERS = 3
TILE = 128
FEAT = 256
CONFIDENCE = 8.0
RIDGE = 0.1
MESH = pl.DeviceIdType.MESH

PART_ROWS = (48, 40, 40)
PART_FIRST = (0, 48, 88)
ROUTES = (("x", "y", "z"), ("y", "z", "x"), ("z", "x", "y"))
PARTS = 3
SIDE = 4
CORES = 2
HALF = IB_DEV // 2
PLANE = SIDE * SIDE * IB_DEV
CHUNK = 8
BUFFERS = 3
USUAL = 40
MOST = 64


def route_of(p, core):
    return ROUTES[(p + core) % PARTS]


def my_coords():
    shard = lax.axis_index("shard")
    return {
        "z": lax.axis_index("group"),
        "y": shard // (SIDE * CORES),
        "x": (shard // CORES) % SIDE,
        "core": shard % CORES,
    }


def device_at(coords):
    return (coords["z"], (coords["y"] * SIDE + coords["x"]) * CORES + coords["core"])


def shifted(coords, axis, offset):
    moved = dict(coords)
    moved[axis] = (coords[axis] + offset) % (CORES if axis == "core" else SIDE)
    return moved


def place(coords, p, turn):
    core = coords["core"]
    return coords[route_of(p, 0)[turn]] * (1 - core) + coords[route_of(p, 1)[turn]] * core


def along(coords, p, turn, offset):
    core = coords["core"]
    moved = dict(coords)
    for axis, here in ((route_of(p, 0)[turn], 1 - core), (route_of(p, 1)[turn], core)):
        moved[axis] = (coords[axis] + offset * here) % SIDE
    return device_at(moved)


def split(values):
    high = values.astype(jnp.bfloat16)
    return high, (values - high.astype(jnp.float32)).astype(jnp.bfloat16)


def dot(left, right):
    return lax.dot_general(left, right, (((1,), (0,)), ((), ())), preferred_element_type=jnp.float32)


def exchange_kernel(cap, piece, with_gram, items_ref, lists_ref, over_ref, r0_ref, r1_ref, r2_ref, gram_ref,
                    p0_ref, p1_ref, p2_ref, s0_ref, s1_ref, s2_ref, asked_ref, asked_smem, own_sem, smem_sem,
                    list_send, list_recv, first_send, first_recv, second_send, second_recv, third_send,
                    third_recv, side_send, side_recv, keep_sem, items_vmem, x_out, x_in, y_out, y_in, z_out, z_in,
                    core_out, core_in, gram_send, gram_recv):
    received = (r0_ref, r1_ref, r2_ref)
    planes = (p0_ref, p1_ref, p2_ref)
    staged = (s0_ref, s1_ref, s2_ref)
    pieces = cap // piece
    me = my_coords()
    sibling = device_at(shifted(me, "core", 1))

    barrier = pltpu.get_barrier_semaphore()
    for axis in ("x", "y", "z"):
        for offset in (1, 2, 3):
            pl.semaphore_signal(barrier, inc=1, device_id=device_at(shifted(me, axis, offset)), device_id_type=MESH)
    pl.semaphore_signal(barrier, inc=1, device_id=sibling, device_id_type=MESH)

    loads = []
    for p in range(PARTS):
        own = (place(me, p, 1) * SIDE + place(me, p, 0)) * IB_DEV
        loads.append(
            pltpu.make_async_copy(
                items_ref.at[:, pl.ds(PART_FIRST[p], PART_ROWS[p]), :],
                planes[p].at[pl.ds(own, IB_DEV)],
                own_sem.at[p],
            )
        )
        loads[p].start()
    items_load = pltpu.make_async_copy(items_ref, items_vmem, own_sem.at[PARTS])
    items_load.start()
    pl.semaphore_wait(barrier, 10)

    list_copies = []
    for p in range(PARTS):
        for offset in (1, 2, 3):
            slot = SIDE - offset
            copy = pltpu.make_async_remote_copy(
                src_ref=lists_ref.at[p, (place(me, p, 2) + offset) % SIDE],
                dst_ref=asked_ref.at[p, slot],
                send_sem=list_send.at[p, slot],
                recv_sem=list_recv.at[p, slot],
                device_id=along(me, p, 2, offset),
                device_id_type=MESH,
            )
            copy.start()
            list_copies.append(copy)

    def plane_copy(p, db, da, half, turn, offset, send_sem, recv_sem):
        at = (((place(me, p, 1) + db) % SIDE) * SIDE + (place(me, p, 0) + da) % SIDE) * IB_DEV
        if half is None:
            where = pl.ds(at, IB_DEV)
        else:
            where = pl.ds(at + half * HALF, HALF)
        return pltpu.make_async_remote_copy(
            src_ref=planes[p].at[where],
            dst_ref=planes[p].at[where],
            send_sem=send_sem,
            recv_sem=recv_sem,
            device_id=along(me, p, turn, offset),
            device_id_type=MESH,
        )

    def first(p, slot):
        da, half, offset = ((0, None, 1), (0, None, 3), (3, 0, 1), (1, 1, 3))[slot]
        return plane_copy(p, 0, da, half, 0, offset, first_send.at[p, slot], first_recv.at[p, slot])

    def second(p, da, slot):
        db, half, offset = ((0, None, 1), (0, None, 3), (3, 0, 1), (1, 1, 3))[slot]
        return plane_copy(
            p, db, da, half, 1, offset, second_send.at[p, da, slot], second_recv.at[p, da, slot]
        )

    quarter, sixteenth = FEAT // SIDE, FEAT // SIDE // SIDE

    def gram_copy(stage, axis, offset, source, target):
        return pltpu.make_async_remote_copy(
            src_ref=source,
            dst_ref=target,
            send_sem=gram_send.at[stage, SIDE - offset],
            recv_sem=gram_recv.at[stage, SIDE - offset],
            device_id=device_at(shifted(me, axis, offset)),
            device_id_type=MESH,
        )

    def gram_copies(stage):
        if stage == 0:
            return [gram_copy(0, "x", o, x_out.at[(me["x"] + o) % SIDE], x_in.at[SIDE - o]) for o in (1, 2, 3)]
        if stage == 1:
            return [gram_copy(1, "y", o, y_out.at[(me["y"] + o) % SIDE], y_in.at[SIDE - o]) for o in (1, 2, 3)]
        if stage == 2:
            return [gram_copy(2, "z", o, z_out, z_in.at[SIDE - o]) for o in (1, 2, 3)]
        if stage == 3:
            return [gram_copy(3, "core", 1, core_out, core_in)]
        if stage == 4:
            rows = gram_ref.at[pl.ds(me["x"] * quarter + me["y"] * sixteenth, sixteenth)]
            return [gram_copy(4, "y", o, rows, rows) for o in (1, 2, 3)]
        rows = gram_ref.at[pl.ds(me["x"] * quarter, quarter)]
        return [gram_copy(5, "x", o, rows, rows) for o in (1, 2, 3)]

    def gram_step(stage):
        if not with_gram:
            return
        if stage > 0:
            for copy in gram_copies(stage - 1):
                copy.wait_recv()
        if stage == 0:
            items_load.wait()

            def add_block(i, running):
                high, low = split(items_vmem[i])
                high_t = high.T
                both = dot(jnp.concatenate([high_t, low.T], axis=0), high)
                return running + both[:FEAT] + both[FEAT:] + dot(high_t, low)

            local = lax.fori_loop(0, IB_DEV, add_block, jnp.zeros((FEAT, FEAT), jnp.float32))
            for i in range(SIDE):
                x_out[i, :quarter] = local[i * quarter:(i + 1) * quarter]
                x_out[i, quarter:] = over_ref[...]
        elif stage == 1:
            total = x_out[me["x"]] + x_in[1] + x_in[2] + x_in[3]
            for i in range(SIDE):
                y_out[i, :sixteenth] = total[i * sixteenth:(i + 1) * sixteenth]
                y_out[i, sixteenth:] = total[quarter:]
        elif stage == 2:
            z_out[...] = y_out[me["y"]] + y_in[1] + y_in[2] + y_in[3]
        elif stage == 3:
            core_out[...] = z_out[...] + z_in[1] + z_in[2] + z_in[3]
        elif stage == 4:
            total = core_out[...] + core_in[...]
            gram_ref[pl.ds(me["x"] * quarter + me["y"] * sixteenth, sixteenth)] = total[:sixteenth]
            gram_ref[pl.ds(FEAT, 8)] = total[sixteenth:]
        if stage < 6:
            for copy in gram_copies(stage):
                copy.start()

    for p in range(PARTS):
        loads[p].wait()
        first(p, 0).start()
        first(p, 1).start()
        second(p, 0, 0).start()
        second(p, 0, 1).start()
    gram_step(0)
    for p in range(PARTS):
        first(p, 0).wait_recv()
        first(p, 2).start()
        second(p, 3, 0).start()
        second(p, 3, 1).start()
        first(p, 1).wait_recv()
        first(p, 3).start()
        second(p, 1, 0).start()
        second(p, 1, 1).start()
    for p in range(PARTS):
        second(p, 0, 0).wait_recv()
        second(p, 0, 2).start()
        second(p, 0, 1).wait_recv()
        second(p, 0, 3).start()
    gram_step(1)
    for p in range(PARTS):
        first(p, 2).wait_recv()
        first(p, 3).wait_recv()
        second(p, 2, 0).start()
        second(p, 2, 1).start()
    gram_step(2)
    for da in (3, 1, 2):
        for p in range(PARTS):
            second(p, da, 0).wait_recv()
            second(p, da, 2).start()
            second(p, da, 1).wait_recv()
            second(p, da, 3).start()
        if da != 2:
            gram_step({3: 3, 1: 4}[da])

    for copy in list_copies:
        copy.wait()
    for p in range(PARTS):
        for offset in range(SIDE):
            source = lists_ref.at[p, place(me, p, 2)] if offset == 0 else asked_ref.at[p, offset]
            copy = pltpu.make_async_copy(source, asked_smem.at[p, offset], smem_sem.at[p, offset])
            copy.start()
    for p in range(PARTS):
        for offset in range(SIDE):
            pltpu.make_async_copy(lists_ref.at[p, 0], asked_smem.at[p, offset], smem_sem.at[p, offset]).wait()
    gram_step(5)

    def slots_of(p, offset, core, start):
        at = ((place(me, p, 2) + offset) % SIDE * CORES + core) * MOST
        return pl.ds(at + start, piece)

    def third(p, offset, i):
        return pltpu.make_async_remote_copy(
            src_ref=staged[p].at[offset, pl.ds(i * piece, piece)],
            dst_ref=received[p].at[slots_of(p, 0, me["core"], i * piece)],
            send_sem=third_send.at[p, SIDE - offset, i],
            recv_sem=third_recv.at[p, SIDE - offset, i],
            device_id=along(me, p, 2, offset),
            device_id_type=MESH,
        )

    def side(p, offset, i):
        here = received[p].at[slots_of(p, offset, me["core"], i * piece)]
        source = staged[p].at[0, pl.ds(i * piece, piece)] if offset == 0 else here
        return pltpu.make_async_remote_copy(
            src_ref=source,
            dst_ref=here,
            send_sem=side_send.at[p, offset, i],
            recv_sem=side_recv.at[p, offset, i],
            device_id=sibling,
            device_id_type=MESH,
        )

    def keep(p, i):
        return pltpu.make_async_copy(
            staged[p].at[0, pl.ds(i * piece, piece)],
            received[p].at[slots_of(p, 0, me["core"], i * piece)],
            keep_sem.at[p, i],
        )

    def stage(p, offset, i):
        def one(j, carry):
            at = i * piece + j
            staged[p][offset, at] = planes[p][asked_smem[p, offset, 0, at]]
            return carry

        lax.fori_loop(0, piece, one, 0)

    def send_part(p, i):
        for offset in (2, 1, 3):
            stage(p, offset, i)
            third(p, offset, i).start()

    def send_pieces(i, carry):
        for p in range(PARTS):
            send_part(p, i)
        return carry

    for p in range(PARTS):
        for da in (0, 3, 1, 2):
            second(p, da, 2).wait_recv()
            second(p, da, 3).wait_recv()
        send_part(p, 0)
    lax.fori_loop(1, pieces, send_pieces, 0)

    def keep_pieces(i, carry):
        for p in range(PARTS):
            stage(p, 0, i)
            keep(p, i).start()
            side(p, 0, i).start()
        return carry

    lax.fori_loop(0, pieces, keep_pieces, 0)

    def pass_pieces(i, carry):
        for p in range(PARTS):
            for offset in (1, 2, 3):
                third(p, SIDE - offset, i).wait_recv()
                side(p, offset, i).start()
        return carry

    lax.fori_loop(0, pieces, pass_pieces, 0)

    def end_pieces(i, carry):
        for p in range(PARTS):
            keep(p, i).wait()
            for offset in range(SIDE):
                side(p, offset, i).wait()
                if offset:
                    third(p, offset, i).wait_send()
        return carry

    lax.fori_loop(0, pieces, end_pieces, 0)
    gram_step(6)
    if with_gram:
        for stage in range(6):
            for copy in gram_copies(stage):
                copy.wait_send()
    else:
        items_load.wait()
        gram_ref[...] = jnp.zeros_like(gram_ref)
    for p in range(PARTS):
        for slot in range(4):
            first(p, slot).wait_send()
            for da in range(SIDE):
                second(p, da, slot).wait_send()


def exchange(items, lists, over, cap, piece, with_gram, collective_id):
    pieces = cap // piece
    dma = pltpu.SemaphoreType.DMA
    return pl.pallas_call(
        functools.partial(exchange_kernel, cap, piece, with_gram),
        out_shape=[
            jax.ShapeDtypeStruct((SIDE * CORES * MOST, rows, FEAT), jnp.float32) for rows in PART_ROWS
        ]
        + [jax.ShapeDtypeStruct((FEAT + 8, FEAT), jnp.float32)],
        in_specs=[pl.BlockSpec(memory_space=pl.ANY)] + [pl.BlockSpec(memory_space=pltpu.VMEM)] * 2,
        out_specs=[pl.BlockSpec(memory_space=pl.ANY)] * PARTS + [pl.BlockSpec(memory_space=pltpu.VMEM)],
        scratch_shapes=[pltpu.VMEM((PLANE, rows, FEAT), jnp.float32) for rows in PART_ROWS]
        + [pltpu.VMEM((SIDE, cap, rows, FEAT), jnp.float32) for rows in PART_ROWS]
        + [
            pltpu.VMEM((PARTS, SIDE, 8, TILE), jnp.int32),
            pltpu.SMEM((PARTS, SIDE, 8, TILE), jnp.int32),
            dma((PARTS + 1,)),
            dma((PARTS, SIDE)),
            dma((PARTS, SIDE)),
            dma((PARTS, SIDE)),
            dma((PARTS, 4)),
            dma((PARTS, 4)),
            dma((PARTS, SIDE, 4)),
            dma((PARTS, SIDE, 4)),
            dma((PARTS, SIDE, pieces)),
            dma((PARTS, SIDE, pieces)),
            dma((PARTS, SIDE, pieces)),
            dma((PARTS, SIDE, pieces)),
            dma((PARTS, pieces)),
            pltpu.VMEM((IB_DEV, TILE, FEAT), jnp.float32),
            pltpu.VMEM((SIDE, FEAT // SIDE + 8, FEAT), jnp.float32),
            pltpu.VMEM((SIDE, FEAT // SIDE + 8, FEAT), jnp.float32),
            pltpu.VMEM((SIDE, FEAT // SIDE // SIDE + 8, FEAT), jnp.float32),
            pltpu.VMEM((SIDE, FEAT // SIDE // SIDE + 8, FEAT), jnp.float32),
            pltpu.VMEM((FEAT // SIDE // SIDE + 8, FEAT), jnp.float32),
            pltpu.VMEM((SIDE, FEAT // SIDE // SIDE + 8, FEAT), jnp.float32),
            pltpu.VMEM((FEAT // SIDE // SIDE + 8, FEAT), jnp.float32),
            pltpu.VMEM((FEAT // SIDE // SIDE + 8, FEAT), jnp.float32),
            dma((6, SIDE)),
            dma((6, SIDE)),
        ],
        compiler_params=pltpu.CompilerParams(
            collective_id=collective_id, has_side_effects=True, vmem_limit_bytes=60 << 20
        ),
        name=f"exchange_{cap}",
    )(items.reshape(IB_DEV, TILE, FEAT), lists, over)


def split_product(left, high, low):
    rows = left.shape[0]
    left_high, left_low = split(left)
    both = dot(jnp.concatenate([left_high, left_low], axis=0), high)
    return both[:rows] + both[rows:] + dot(left_high, low)


def solve_kernel(first, count, plan_ref, gram_ref, r0_ref, r1_ref, r2_ref, counts_ref,
                 out_ref, order, totals, rows_buf, counts_buf, high_ref, low_ref, high_t_ref, low_t_ref, weight_ref, sems):
    received = (r0_ref, r1_ref, r2_ref)

    step_at = pl.program_id(0)

    @pl.when(step_at == 0)
    def _():
        for own in range(count):

            def append(k, total, own=own):
                order[own, total] = k
                return total + (plan_ref[PARTS, k] == first + own).astype(jnp.int32)

            totals[own] = lax.fori_loop(0, TILE, append, 0, unroll=8)

    total = totals[step_at]
    chunks = (total + CHUNK - 1) // CHUNK

    def copies(at, i, slot):
        result = []
        for t in range(CHUNK):
            k = order[at, jnp.minimum(i * CHUNK + t, totals[at] - 1)]
            for p in range(PARTS):
                result.append(
                    pltpu.make_async_copy(
                        received[p].at[plan_ref[p, k]],
                        rows_buf.at[slot, pl.ds(t * TILE + PART_FIRST[p], PART_ROWS[p])],
                        sems.at[slot, 0],
                    )
                )
            result.append(pltpu.make_async_copy(counts_ref.at[k], counts_buf.at[slot, t], sems.at[slot, 1]))
        return result

    def fetch(at, i):
        @pl.when(i * CHUNK < totals[at])
        def _():
            for copy in copies(at, i, lax.rem(i, BUFFERS)):
                copy.start()

    @pl.when(step_at == 0)
    def _():
        for i in range(BUFFERS - 1):
            fetch(0, i)

    def load(i, right):
        slot = lax.rem(i, BUFFERS)
        fetch(step_at, i + BUFFERS - 1)
        pltpu.make_async_copy(rows_buf.at[slot], rows_buf.at[slot], sems.at[slot, 0]).wait()
        pltpu.make_async_copy(counts_buf.at[slot], counts_buf.at[slot], sems.at[slot, 1]).wait()
        high, low = split(rows_buf[slot])
        high_ref[i] = high
        low_ref[i] = low
        high_t_ref[i] = high.T
        low_t_ref[i] = low.T
        ones = []
        for t in range(CHUNK):
            live = (i * CHUNK + t < total).astype(jnp.float32)
            weight = counts_buf[slot, t].astype(jnp.float32) * (CONFIDENCE * live)
            weight_ref[i, :, t * TILE:(t + 1) * TILE] = weight.astype(jnp.bfloat16)
            ones.append((weight + live).astype(jnp.bfloat16))
        ones = jnp.concatenate(ones, axis=1)
        return right + dot(ones, high) + dot(ones, low)

    right = lax.fori_loop(0, chunks, load, jnp.zeros((TILE, FEAT), jnp.float32))

    @pl.when(step_at + 1 < count)
    def _():
        for i in range(BUFFERS - 1):
            fetch(step_at + 1, i)

    gram_high, gram_low = split(gram_ref[:FEAT])

    solved = jnp.zeros_like(right)
    residual = right
    direction = right
    norm_now = jnp.sum(residual * residual, axis=-1, keepdims=True)
    for iteration in range(CG_ITERS):
        base = split_product(direction, gram_high, gram_low) + RIDGE * direction
        if iteration < CG_ITERS - 1:

            def scaled(i):
                scores = split_product(direction, high_t_ref[i], low_t_ref[i])
                return split(scores * weight_ref[i].astype(jnp.float32))

            def image_of(halves, i):
                both = dot(jnp.concatenate(halves, axis=0), high_ref[i])
                return both[:TILE] + both[TILE:] + dot(halves[0], low_ref[i])

            def apply(i, carry):
                running, high, low = carry
                running = running + image_of((high, low), i - 1)
                return (running,) + scaled(i)

            image, last_high, last_low = lax.fori_loop(1, chunks, apply, (base,) + scaled(0))
            image = image + image_of((last_high, last_low), chunks - 1)
            curve = jnp.sum(direction * image, axis=-1, keepdims=True)
        else:
            direction_halves = jnp.concatenate(split(direction), axis=0)

            def scores_of(i):
                both = dot(direction_halves, high_t_ref[i])
                return both[:TILE] + both[TILE:]

            def energy_of(scores, i):
                terms = scores * scores * weight_ref[i].astype(jnp.float32)
                parts = [terms[:, t * TILE:(t + 1) * TILE] for t in range(CHUNK)]
                return sum(parts[1:], parts[0])

            def energy(i, carry):
                running, scores = carry
                return running + energy_of(scores, i - 1), scores_of(i)

            initial = jnp.zeros((TILE, TILE), jnp.float32)
            energies, last_scores = lax.fori_loop(1, chunks, energy, (initial, scores_of(0)))
            energies = energies + energy_of(last_scores, chunks - 1)
            curve = jnp.sum(direction * base, axis=-1, keepdims=True) + jnp.sum(energies, axis=-1, keepdims=True)
        step = norm_now / curve
        solved = solved + step * direction
        if iteration < CG_ITERS - 1:
            residual = residual - step * image
            norm_next = jnp.sum(residual * residual, axis=-1, keepdims=True)
            direction = residual + norm_next / norm_now * direction
            norm_now = norm_next
    out_ref[...] = solved


def solve(first, count, places, gram, received, counts):
    smem = pl.BlockSpec(memory_space=pltpu.SMEM)
    vmem = pl.BlockSpec(memory_space=pltpu.VMEM)
    hbm = pl.BlockSpec(memory_space=pl.ANY)
    most = TILE // CHUNK
    return pl.pallas_call(
        functools.partial(solve_kernel, first, count),
        grid=(count,),
        out_shape=jax.ShapeDtypeStruct((count * TILE, FEAT), jnp.float32),
        in_specs=[smem, vmem] + [hbm] * 4,
        out_specs=pl.BlockSpec((TILE, FEAT), lambda b: (b, 0)),
        scratch_shapes=[
            pltpu.SMEM((count, TILE), jnp.int32),
            pltpu.SMEM((count,), jnp.int32),
            pltpu.VMEM((BUFFERS, CHUNK * TILE, FEAT), jnp.float32),
            pltpu.VMEM((BUFFERS, CHUNK, TILE, TILE), jnp.int32),
            pltpu.VMEM((most, CHUNK * TILE, FEAT), jnp.bfloat16),
            pltpu.VMEM((most, CHUNK * TILE, FEAT), jnp.bfloat16),
            pltpu.VMEM((most, FEAT, CHUNK * TILE), jnp.bfloat16),
            pltpu.VMEM((most, FEAT, CHUNK * TILE), jnp.bfloat16),
            pltpu.VMEM((most, TILE, CHUNK * TILE), jnp.bfloat16),
            pltpu.SemaphoreType.DMA((BUFFERS, 2)),
        ],
        cost_estimate=pl.CostEstimate(flops=8_000_000_000, bytes_accessed=16 << 20, transcendentals=0),
        compiler_params=pltpu.CompilerParams(vmem_limit_bytes=56 << 20),
        name=f"solve_{first}",
    )(places, gram, *received, counts)


def share_kernel(mine_ref, out_ref, send, recv, keep):
    me = my_coords()
    barrier = pltpu.get_barrier_semaphore()
    for offset in (1, 2, 3):
        pl.semaphore_signal(barrier, inc=1, device_id=device_at(shifted(me, "z", offset)), device_id_type=MESH)
    own = pltpu.make_async_copy(mine_ref, out_ref.at[me["z"]], keep)
    own.start()
    pl.semaphore_wait(barrier, 3)
    remotes = [
        pltpu.make_async_remote_copy(
            src_ref=mine_ref,
            dst_ref=out_ref.at[me["z"]],
            send_sem=send.at[offset],
            recv_sem=recv.at[offset],
            device_id=device_at(shifted(me, "z", offset)),
            device_id_type=MESH,
        )
        for offset in (1, 2, 3)
    ]
    for copy in remotes:
        copy.start()
    own.wait()
    for copy in remotes:
        copy.wait()


def share(mine):
    return pl.pallas_call(
        share_kernel,
        out_shape=jax.ShapeDtypeStruct((SIDE,) + mine.shape, jnp.float32),
        in_specs=[pl.BlockSpec(memory_space=pltpu.VMEM)],
        out_specs=pl.BlockSpec(memory_space=pltpu.VMEM),
        scratch_shapes=[
            pltpu.SemaphoreType.DMA((SIDE,)),
            pltpu.SemaphoreType.DMA((SIDE,)),
            pltpu.SemaphoreType.DMA,
        ],
        compiler_params=pltpu.CompilerParams(collective_id=2, has_side_effects=True),
        name="share",
    )(mine)


def plan(blocks_row, users_row, live_count, core):
    slots = blocks_row.shape[0]
    shard_size = lax.axis_size("shard")
    asked = jnp.where(jnp.arange(slots) < live_count, blocks_row, -1)
    other = lax.ppermute(asked, "shard", [(s, s ^ 1) for s in range(shard_size)])
    both = jnp.concatenate([asked, other])
    block_total = SIDE * SIDE * SIDE * CORES * IB_DEV
    needed = jnp.any(both[:, None] == jnp.arange(block_total)[None, :], axis=0)
    needed = needed.astype(jnp.float32).reshape(SIDE, SIDE, SIDE, CORES, IB_DEV)
    axes = {"z": 0, "y": 1, "x": 2}
    turns = {(p, k): [axes[axis] for axis in route_of(p, k)] for p in range(PARTS) for k in range(CORES)}
    ordered = jnp.stack([
        jnp.stack([
            jnp.transpose(needed[:, :, :, k], turns[p, k][::-1] + [3]).reshape(SIDE, PLANE) for k in range(CORES)
        ])
        for p in range(PARTS)
    ])
    before = (jnp.arange(PLANE)[:, None] < jnp.arange(PLANE)[None, :]).astype(jnp.float32)
    rank = jnp.einsum("pksi,ij->pksj", ordered, before, preferred_element_type=jnp.float32).astype(jnp.int32)
    most = jnp.max(jnp.sum(ordered, axis=-1))
    mine = lax.dynamic_index_in_dim(ordered, core, 1, keepdims=False) > 0
    mine_rank = lax.dynamic_index_in_dim(rank, core, 1, keepdims=False)
    hits = jnp.logical_and(mine[:, :, None, :], mine_rank[:, :, None, :] == jnp.arange(TILE)[:, None])
    lists = jnp.sum(jnp.where(hits, jnp.arange(PLANE, dtype=jnp.int32), 0), axis=-1)
    lists = jnp.broadcast_to(lists[:, :, None, :], (PARTS, SIDE, 8, TILE))
    tables = []
    for p in range(PARTS):
        sides = []
        for k in range(CORES):
            back = [turns[p, k][::-1].index(axis) for axis in range(3)] + [3]
            sides.append(jnp.transpose(rank[p, k].reshape(SIDE, SIDE, SIDE, IB_DEV), back))
        tables.append(jnp.stack(sides, axis=3).reshape(block_total))
    ranks = jnp.stack(tables)
    block = jnp.arange(block_total)
    where = {"z": block // 256, "y": block // 64 % 4, "x": block // 16 % 4}
    source_core = block // IB_DEV % CORES
    source = jnp.stack([
        jnp.where(source_core == 0, where[route_of(p, 0)[2]], where[route_of(p, 1)[2]]) * CORES + source_core
        for p in range(PARTS)
    ])
    table = source * MOST + jnp.minimum(ranks, MOST - 1)
    picked = blocks_row[:, None] == block[None, :]
    places = jnp.sum(jnp.where(picked[None], table[:, None, :], 0), axis=-1)
    users = jnp.where(jnp.arange(slots) < live_count, users_row, UB_DEV)
    places = jnp.concatenate([places, users[None], jnp.zeros((8 - PARTS - 1, slots), jnp.int32)])
    return lists, places, most


def body(item_factors, item_block, tile_user, tile_count, tile_counts):
    blocks_row = item_block[0]
    users_row = tile_user[0]
    core = lax.axis_index("shard") % CORES
    lists, places, most = plan(blocks_row, users_row, tile_count[0], core)
    over = jnp.full((8, FEAT), (most > USUAL).astype(jnp.float32))
    *received, gram = exchange(item_factors, lists, over, USUAL, 8, True, 0)
    again = gram[FEAT, 0] > 0
    _, received = lax.while_loop(
        lambda carry: carry[0],
        lambda carry: (jnp.zeros_like(again), tuple(exchange(item_factors, lists, over, MOST, 16, False, 1)[:PARTS])),
        (again, tuple(received)),
    )
    half = UB_DEV // 2
    earlier = solve(0, half, places, gram, received, tile_counts)
    earlier = lax.all_gather(earlier, "group", axis=0)
    later = solve(half, half, places, gram, received, tile_counts)
    return jnp.concatenate([earlier, share(later)], axis=1).reshape(-1, FEAT)


def solution(mesh):
    return jax.shard_map(
        body,
        mesh=mesh,
        in_specs=(
            P(("group", "shard"), None),
            P(("group", "shard"), None),
            P(("group", "shard"), None),
            P(("group", "shard")),
            P(("group", "shard"), None, None),
        ),
        out_specs=P("shard", None),
        check_vma=False,
    )
```

```python
import functools

import jax
import jax.numpy as jnp
from jax import lax
from jax.experimental import pallas as pl
from jax.experimental.pallas import tpu as pltpu
from jax.sharding import PartitionSpec as P

UB_DEV = 4
IB_DEV = 8
CG_ITERS = 3
TILE = 128
FEAT = 256
CONFIDENCE = 8.0
RIDGE = 0.1
MESH = pl.DeviceIdType.MESH

PART_ROWS = (48, 40, 40)
PART_FIRST = (0, 48, 88)
ROUTES = (("x", "y", "z"), ("y", "z", "x"), ("z", "x", "y"))
PARTS = 3
SIDE = 4
CORES = 2
HALF = IB_DEV // 2
PLANE = SIDE * SIDE * IB_DEV
CHUNK = 8
BUFFERS = 3
USUAL = 40
MOST = 64


def route_of(p, core):
    return ROUTES[(p + core) % PARTS]


def my_coords():
    shard = lax.axis_index("shard")
    return {
        "z": lax.axis_index("group"),
        "y": shard // (SIDE * CORES),
        "x": (shard // CORES) % SIDE,
        "core": shard % CORES,
    }


def device_at(coords):
    return (coords["z"], (coords["y"] * SIDE + coords["x"]) * CORES + coords["core"])


def shifted(coords, axis, offset):
    moved = dict(coords)
    moved[axis] = (coords[axis] + offset) % (CORES if axis == "core" else SIDE)
    return moved


def place(coords, p, turn):
    core = coords["core"]
    return coords[route_of(p, 0)[turn]] * (1 - core) + coords[route_of(p, 1)[turn]] * core


def along(coords, p, turn, offset):
    core = coords["core"]
    moved = dict(coords)
    for axis, here in ((route_of(p, 0)[turn], 1 - core), (route_of(p, 1)[turn], core)):
        moved[axis] = (coords[axis] + offset * here) % SIDE
    return device_at(moved)


def split(values):
    high = values.astype(jnp.bfloat16)
    return high, (values - high.astype(jnp.float32)).astype(jnp.bfloat16)


def dot(left, right):
    return lax.dot_general(left, right, (((1,), (0,)), ((), ())), preferred_element_type=jnp.float32)


def dot_t(left, right):
    return lax.dot_general(left, right, (((1,), (1,)), ((), ())), preferred_element_type=jnp.float32)


def code_of(block, p):
    at = {"z": block >> 8 & 3, "y": block >> 6 & 3, "x": block >> 4 & 3}
    core = block >> 3 & 1
    codes = []
    for k in range(CORES):
        a, b, c = route_of(p, k)
        codes.append(((k * SIDE + at[c]) * SIDE + at[b]) * SIDE + at[a])
    return jnp.where(core == 0, codes[0], codes[1]) * IB_DEV + (block & 7)


def write_plan(ids, other, core, lists_ref, places_ref):
    across = lax.broadcasted_iota(jnp.int32, (TILE, TILE), 1)
    down = lax.broadcasted_iota(jnp.int32, (TILE, TILE), 0)
    block_total = SIDE * SIDE * SIDE * CORES * IB_DEV
    codes = lax.broadcasted_iota(jnp.int32, (TILE, block_total), 1)

    def column(row):
        return jnp.sum(jnp.where(across == down, row, 0), axis=1, keepdims=True)

    own_row = ids[:1]
    own_column, other_column = column(own_row), column(other[:1])
    before = (down < across).astype(jnp.bfloat16)
    values = lax.broadcasted_iota(jnp.int32, (8, TILE), 1).astype(jnp.bfloat16)
    place_rows = []
    longest = jnp.zeros((1, 1), jnp.float32)
    for p in range(PARTS):
        own_code = jnp.where(own_column < 0, -1, code_of(own_column, p))
        other_code = jnp.where(other_column < 0, -1, code_of(other_column, p))
        own_hits = own_code == codes
        hits = jnp.logical_or(own_hits, other_code == codes).astype(jnp.float32)
        needed = jnp.max(hits, axis=0, keepdims=True)
        needed = jnp.concatenate([needed[:, i * TILE:(i + 1) * TILE] for i in range(CORES * SIDE)], axis=0)
        rank = dot(needed.astype(jnp.bfloat16), before)
        longest = jnp.maximum(longest, jnp.max(jnp.sum(needed, axis=1, keepdims=True), axis=0, keepdims=True))
        mine = jnp.where(core == 0, needed[:SIDE], needed[SIDE:])
        mine_rank = jnp.where(core == 0, rank[:SIDE], rank[SIDE:]).astype(jnp.int32)
        for t in range(SIDE):
            chosen = jnp.logical_and(mine_rank[t:t + 1] == down, mine[t:t + 1] > 0).astype(jnp.bfloat16)
            lists_ref[p, t] = jnp.clip(dot_t(values, chosen).astype(jnp.int32), 0, PLANE - 1)
        flat = jnp.concatenate([rank[i:i + 1] for i in range(CORES * SIDE)], axis=1)
        flat = jnp.broadcast_to(flat, (8, block_total)).astype(jnp.bfloat16)
        own_rank = dot_t(flat, own_hits.astype(jnp.bfloat16))[:1].astype(jnp.int32)
        row_code = code_of(own_row, p)
        source = (row_code >> 7 & 3) * CORES + (row_code >> 9 & 1)
        place_rows.append(source * MOST + jnp.clip(own_rank, 0, MOST - 1))
    places_ref[...] = jnp.concatenate(place_rows + [ids[1:2], jnp.zeros((8 - PARTS - 1, TILE), jnp.int32)], axis=0)
    return jnp.broadcast_to(jnp.where(longest > USUAL, 1.0, 0.0), (8, FEAT))


def exchange_kernel(cap, piece, with_gram, items_ref, ids_ref, r0_ref, r1_ref, r2_ref, gram_ref, places_ref,
                    p0_ref, p1_ref, p2_ref, s0_ref, s1_ref, s2_ref, asked_ref, asked_smem, own_sem, smem_sem,
                    list_send, list_recv, first_send, first_recv, second_send, second_recv, third_send,
                    third_recv, side_send, side_recv, keep_sem, items_vmem, x_out, x_in, y_out, y_in, z_out, z_in,
                    core_out, core_in, gram_send, gram_recv, other_ref, lists_ref, other_sem):
    received = (r0_ref, r1_ref, r2_ref)
    planes = (p0_ref, p1_ref, p2_ref)
    staged = (s0_ref, s1_ref, s2_ref)
    pieces = cap // piece
    me = my_coords()
    sibling = device_at(shifted(me, "core", 1))

    barrier = pltpu.get_barrier_semaphore()
    for axis in ("x", "y", "z"):
        for offset in (1, 2, 3):
            pl.semaphore_signal(barrier, inc=1, device_id=device_at(shifted(me, axis, offset)), device_id_type=MESH)
    pl.semaphore_signal(barrier, inc=1, device_id=sibling, device_id_type=MESH)

    loads = []
    for p in range(PARTS):
        own = (place(me, p, 1) * SIDE + place(me, p, 0)) * IB_DEV
        loads.append(
            pltpu.make_async_copy(
                items_ref.at[:, pl.ds(PART_FIRST[p], PART_ROWS[p]), :],
                planes[p].at[pl.ds(own, IB_DEV)],
                own_sem.at[p],
            )
        )
        loads[p].start()
    items_load = pltpu.make_async_copy(items_ref, items_vmem, own_sem.at[PARTS])
    items_load.start()
    pl.semaphore_wait(barrier, 10)

    ids_copy = pltpu.make_async_remote_copy(
        src_ref=ids_ref,
        dst_ref=other_ref,
        send_sem=other_sem.at[0],
        recv_sem=other_sem.at[1],
        device_id=sibling,
        device_id_type=MESH,
    )
    ids_copy.start()

    def plane_copy(p, db, da, half, turn, offset, send_sem, recv_sem):
        at = (((place(me, p, 1) + db) % SIDE) * SIDE + (place(me, p, 0) + da) % SIDE) * IB_DEV
        if half is None:
            where = pl.ds(at, IB_DEV)
        else:
            where = pl.ds(at + half * HALF, HALF)
        return pltpu.make_async_remote_copy(
            src_ref=planes[p].at[where],
            dst_ref=planes[p].at[where],
            send_sem=send_sem,
            recv_sem=recv_sem,
            device_id=along(me, p, turn, offset),
            device_id_type=MESH,
        )

    def first(p, slot):
        da, half, offset = ((0, None, 1), (0, None, 3), (3, 0, 1), (1, 1, 3))[slot]
        return plane_copy(p, 0, da, half, 0, offset, first_send.at[p, slot], first_recv.at[p, slot])

    def second(p, da, slot):
        db, half, offset = ((0, None, 1), (0, None, 3), (3, 0, 1), (1, 1, 3))[slot]
        return plane_copy(
            p, db, da, half, 1, offset, second_send.at[p, da, slot], second_recv.at[p, da, slot]
        )

    quarter, sixteenth = FEAT // SIDE, FEAT // SIDE // SIDE

    def gram_copy(stage, axis, offset, source, target):
        return pltpu.make_async_remote_copy(
            src_ref=source,
            dst_ref=target,
            send_sem=gram_send.at[stage, SIDE - offset],
            recv_sem=gram_recv.at[stage, SIDE - offset],
            device_id=device_at(shifted(me, axis, offset)),
            device_id_type=MESH,
        )

    def gram_copies(stage):
        if stage == 0:
            return [gram_copy(0, "x", o, x_out.at[(me["x"] + o) % SIDE], x_in.at[SIDE - o]) for o in (1, 2, 3)]
        if stage == 1:
            return [gram_copy(1, "y", o, y_out.at[(me["y"] + o) % SIDE], y_in.at[SIDE - o]) for o in (1, 2, 3)]
        if stage == 2:
            return [gram_copy(2, "z", o, z_out, z_in.at[SIDE - o]) for o in (1, 2, 3)]
        if stage == 3:
            return [gram_copy(3, "core", 1, core_out, core_in)]
        if stage == 4:
            rows = gram_ref.at[pl.ds(me["x"] * quarter + me["y"] * sixteenth, sixteenth)]
            return [gram_copy(4, "y", o, rows, rows) for o in (1, 2, 3)]
        rows = gram_ref.at[pl.ds(me["x"] * quarter, quarter)]
        return [gram_copy(5, "x", o, rows, rows) for o in (1, 2, 3)]

    def gram_step(stage):
        if not with_gram:
            return
        if stage > 0:
            for copy in gram_copies(stage - 1):
                copy.wait_recv()
        if stage == 0:
            items_load.wait()

            def add_block(i, running):
                high, low = split(items_vmem[i])
                high_t = high.T
                both = dot(jnp.concatenate([high_t, low.T], axis=0), high)
                return running + both[:FEAT] + both[FEAT:] + dot(high_t, low)

            local = lax.fori_loop(0, IB_DEV, add_block, jnp.zeros((FEAT, FEAT), jnp.float32))
            for i in range(SIDE):
                x_out[i, :quarter] = local[i * quarter:(i + 1) * quarter]
                x_out[i, quarter:] = over
        elif stage == 1:
            total = x_out[me["x"]] + x_in[1] + x_in[2] + x_in[3]
            for i in range(SIDE):
                y_out[i, :sixteenth] = total[i * sixteenth:(i + 1) * sixteenth]
                y_out[i, sixteenth:] = total[quarter:]
        elif stage == 2:
            z_out[...] = y_out[me["y"]] + y_in[1] + y_in[2] + y_in[3]
        elif stage == 3:
            core_out[...] = z_out[...] + z_in[1] + z_in[2] + z_in[3]
        elif stage == 4:
            total = core_out[...] + core_in[...]
            gram_ref[pl.ds(me["x"] * quarter + me["y"] * sixteenth, sixteenth)] = total[:sixteenth]
            gram_ref[pl.ds(FEAT, 8)] = total[sixteenth:]
        if stage < 6:
            for copy in gram_copies(stage):
                copy.start()

    for p in range(PARTS):
        loads[p].wait()
        first(p, 0).start()
        first(p, 1).start()
        second(p, 0, 0).start()
        second(p, 0, 1).start()
    ids_copy.wait()
    over = write_plan(ids_ref[...], other_ref[...], me["core"], lists_ref, places_ref)
    list_copies = []
    for p in range(PARTS):
        for offset in (1, 2, 3):
            slot = SIDE - offset
            copy = pltpu.make_async_remote_copy(
                src_ref=lists_ref.at[p, (place(me, p, 2) + offset) % SIDE],
                dst_ref=asked_ref.at[p, slot],
                send_sem=list_send.at[p, slot],
                recv_sem=list_recv.at[p, slot],
                device_id=along(me, p, 2, offset),
                device_id_type=MESH,
            )
            copy.start()
            list_copies.append(copy)
    gram_step(0)
    for p in range(PARTS):
        first(p, 0).wait_recv()
        first(p, 2).start()
        second(p, 3, 0).start()
        second(p, 3, 1).start()
        first(p, 1).wait_recv()
        first(p, 3).start()
        second(p, 1, 0).start()
        second(p, 1, 1).start()
    for p in range(PARTS):
        second(p, 0, 0).wait_recv()
        second(p, 0, 2).start()
        second(p, 0, 1).wait_recv()
        second(p, 0, 3).start()
    gram_step(1)
    for p in range(PARTS):
        first(p, 2).wait_recv()
        first(p, 3).wait_recv()
        second(p, 2, 0).start()
        second(p, 2, 1).start()
    gram_step(2)
    for da in (3, 1, 2):
        for p in range(PARTS):
            second(p, da, 0).wait_recv()
            second(p, da, 2).start()
            second(p, da, 1).wait_recv()
            second(p, da, 3).start()
        if da != 2:
            gram_step({3: 3, 1: 4}[da])

    for copy in list_copies:
        copy.wait()
    for p in range(PARTS):
        for offset in range(SIDE):
            source = lists_ref.at[p, place(me, p, 2)] if offset == 0 else asked_ref.at[p, offset]
            copy = pltpu.make_async_copy(source, asked_smem.at[p, offset], smem_sem.at[p, offset])
            copy.start()
    for p in range(PARTS):
        for offset in range(SIDE):
            pltpu.make_async_copy(lists_ref.at[p, 0], asked_smem.at[p, offset], smem_sem.at[p, offset]).wait()
    gram_step(5)

    def slots_of(p, offset, core, start):
        at = ((place(me, p, 2) + offset) % SIDE * CORES + core) * MOST
        return pl.ds(at + start, piece)

    def third(p, offset, i):
        return pltpu.make_async_remote_copy(
            src_ref=staged[p].at[offset, pl.ds(i * piece, piece)],
            dst_ref=received[p].at[slots_of(p, 0, me["core"], i * piece)],
            send_sem=third_send.at[p, SIDE - offset, i],
            recv_sem=third_recv.at[p, SIDE - offset, i],
            device_id=along(me, p, 2, offset),
            device_id_type=MESH,
        )

    def side(p, offset, i):
        here = received[p].at[slots_of(p, offset, me["core"], i * piece)]
        source = staged[p].at[0, pl.ds(i * piece, piece)] if offset == 0 else here
        return pltpu.make_async_remote_copy(
            src_ref=source,
            dst_ref=here,
            send_sem=side_send.at[p, offset, i],
            recv_sem=side_recv.at[p, offset, i],
            device_id=sibling,
            device_id_type=MESH,
        )

    def keep(p, i):
        return pltpu.make_async_copy(
            staged[p].at[0, pl.ds(i * piece, piece)],
            received[p].at[slots_of(p, 0, me["core"], i * piece)],
            keep_sem.at[p, i],
        )

    def stage(p, offset, i):
        def one(j, carry):
            at = i * piece + j
            block = jnp.minimum(jnp.maximum(asked_smem[p, offset, 0, at], 0), PLANE - 1)
            staged[p][offset, at] = planes[p][block]
            return carry

        lax.fori_loop(0, piece, one, 0)

    def send_part(p, i):
        for offset in (2, 1, 3):
            stage(p, offset, i)
            third(p, offset, i).start()

    def send_pieces(i, carry):
        for p in range(PARTS):
            send_part(p, i)
        return carry

    for p in range(PARTS):
        for da in (0, 3, 1, 2):
            second(p, da, 2).wait_recv()
            second(p, da, 3).wait_recv()
        send_part(p, 0)
    lax.fori_loop(1, pieces, send_pieces, 0)

    def keep_pieces(i, carry):
        for p in range(PARTS):
            stage(p, 0, i)
            keep(p, i).start()
            side(p, 0, i).start()
        return carry

    lax.fori_loop(0, pieces, keep_pieces, 0)

    def pass_pieces(i, carry):
        for p in range(PARTS):
            for offset in (1, 2, 3):
                third(p, SIDE - offset, i).wait_recv()
                side(p, offset, i).start()
        return carry

    lax.fori_loop(0, pieces, pass_pieces, 0)

    def end_pieces(i, carry):
        for p in range(PARTS):
            keep(p, i).wait()
            for offset in range(SIDE):
                side(p, offset, i).wait()
                if offset:
                    third(p, offset, i).wait_send()
        return carry

    lax.fori_loop(0, pieces, end_pieces, 0)
    gram_step(6)
    if with_gram:
        for stage in range(6):
            for copy in gram_copies(stage):
                copy.wait_send()
    else:
        items_load.wait()
        gram_ref[...] = jnp.zeros_like(gram_ref)
    for p in range(PARTS):
        for slot in range(4):
            first(p, slot).wait_send()
            for da in range(SIDE):
                second(p, da, slot).wait_send()


def exchange(items, ids, cap, piece, with_gram, collective_id):
    pieces = cap // piece
    dma = pltpu.SemaphoreType.DMA
    return pl.pallas_call(
        functools.partial(exchange_kernel, cap, piece, with_gram),
        out_shape=[
            jax.ShapeDtypeStruct((SIDE * CORES * MOST, rows, FEAT), jnp.float32) for rows in PART_ROWS
        ]
        + [jax.ShapeDtypeStruct((FEAT + 8, FEAT), jnp.float32), jax.ShapeDtypeStruct((8, TILE), jnp.int32)],
        in_specs=[pl.BlockSpec(memory_space=pl.ANY)] + [pl.BlockSpec(memory_space=pltpu.VMEM)],
        out_specs=[pl.BlockSpec(memory_space=pl.ANY)] * PARTS + [pl.BlockSpec(memory_space=pltpu.VMEM)] * 2,
        scratch_shapes=[pltpu.VMEM((PLANE, rows, FEAT), jnp.float32) for rows in PART_ROWS]
        + [pltpu.VMEM((SIDE, cap, rows, FEAT), jnp.float32) for rows in PART_ROWS]
        + [
            pltpu.VMEM((PARTS, SIDE, 8, TILE), jnp.int32),
            pltpu.SMEM((PARTS, SIDE, 8, TILE), jnp.int32),
            dma((PARTS + 1,)),
            dma((PARTS, SIDE)),
            dma((PARTS, SIDE)),
            dma((PARTS, SIDE)),
            dma((PARTS, 4)),
            dma((PARTS, 4)),
            dma((PARTS, SIDE, 4)),
            dma((PARTS, SIDE, 4)),
            dma((PARTS, SIDE, pieces)),
            dma((PARTS, SIDE, pieces)),
            dma((PARTS, SIDE, pieces)),
            dma((PARTS, SIDE, pieces)),
            dma((PARTS, pieces)),
            pltpu.VMEM((IB_DEV, TILE, FEAT), jnp.float32),
            pltpu.VMEM((SIDE, FEAT // SIDE + 8, FEAT), jnp.float32),
            pltpu.VMEM((SIDE, FEAT // SIDE + 8, FEAT), jnp.float32),
            pltpu.VMEM((SIDE, FEAT // SIDE // SIDE + 8, FEAT), jnp.float32),
            pltpu.VMEM((SIDE, FEAT // SIDE // SIDE + 8, FEAT), jnp.float32),
            pltpu.VMEM((FEAT // SIDE // SIDE + 8, FEAT), jnp.float32),
            pltpu.VMEM((SIDE, FEAT // SIDE // SIDE + 8, FEAT), jnp.float32),
            pltpu.VMEM((FEAT // SIDE // SIDE + 8, FEAT), jnp.float32),
            pltpu.VMEM((FEAT // SIDE // SIDE + 8, FEAT), jnp.float32),
            dma((6, SIDE)),
            dma((6, SIDE)),
            pltpu.VMEM((8, TILE), jnp.int32),
            pltpu.VMEM((PARTS, SIDE, 8, TILE), jnp.int32),
            dma((2,)),
        ],
        compiler_params=pltpu.CompilerParams(
            collective_id=collective_id, has_side_effects=True, vmem_limit_bytes=60 << 20
        ),
        name=f"exchange_{cap}",
    )(items.reshape(IB_DEV, TILE, FEAT), ids)


def split_product(left, high, low):
    rows = left.shape[0]
    left_high, left_low = split(left)
    both = dot(jnp.concatenate([left_high, left_low], axis=0), high)
    return both[:rows] + both[rows:] + dot(left_high, low)


def solve_kernel(first, count, plan_ref, gram_ref, r0_ref, r1_ref, r2_ref, counts_ref,
                 out_ref, order, totals, rows_buf, counts_buf, high_ref, low_ref, high_t_ref, low_t_ref, weight_ref, sems):
    received = (r0_ref, r1_ref, r2_ref)

    step_at = pl.program_id(0)

    @pl.when(step_at == 0)
    def _():
        for own in range(count):

            def append(k, total, own=own):
                order[own, total] = k
                return total + (plan_ref[PARTS, k] == first + own).astype(jnp.int32)

            totals[own] = lax.fori_loop(0, TILE, append, 0, unroll=8)

    total = totals[step_at]
    chunks = (total + CHUNK - 1) // CHUNK

    def copies(at, i, slot):
        result = []
        for t in range(CHUNK):
            k = order[at, jnp.minimum(i * CHUNK + t, totals[at] - 1)]
            for p in range(PARTS):
                result.append(
                    pltpu.make_async_copy(
                        received[p].at[plan_ref[p, k]],
                        rows_buf.at[slot, pl.ds(t * TILE + PART_FIRST[p], PART_ROWS[p])],
                        sems.at[slot, 0],
                    )
                )
            result.append(pltpu.make_async_copy(counts_ref.at[k], counts_buf.at[slot, t], sems.at[slot, 1]))
        return result

    def fetch(at, i):
        @pl.when(i * CHUNK < totals[at])
        def _():
            for copy in copies(at, i, lax.rem(i, BUFFERS)):
                copy.start()

    @pl.when(step_at == 0)
    def _():
        for i in range(BUFFERS - 1):
            fetch(0, i)

    def load(i, right):
        slot = lax.rem(i, BUFFERS)
        fetch(step_at, i + BUFFERS - 1)
        pltpu.make_async_copy(rows_buf.at[slot], rows_buf.at[slot], sems.at[slot, 0]).wait()
        pltpu.make_async_copy(counts_buf.at[slot], counts_buf.at[slot], sems.at[slot, 1]).wait()
        high, low = split(rows_buf[slot])
        high_ref[i] = high
        low_ref[i] = low
        high_t_ref[i] = high.T
        low_t_ref[i] = low.T
        ones = []
        for t in range(CHUNK):
            live = (i * CHUNK + t < total).astype(jnp.float32)
            weight = counts_buf[slot, t].astype(jnp.float32) * (CONFIDENCE * live)
            weight_ref[i, :, t * TILE:(t + 1) * TILE] = weight.astype(jnp.bfloat16)
            ones.append((weight + live).astype(jnp.bfloat16))
        ones = jnp.concatenate(ones, axis=1)
        return right + dot(ones, high) + dot(ones, low)

    right = lax.fori_loop(0, chunks, load, jnp.zeros((TILE, FEAT), jnp.float32))

    @pl.when(step_at + 1 < count)
    def _():
        for i in range(BUFFERS - 1):
            fetch(step_at + 1, i)

    gram_high, gram_low = split(gram_ref[:FEAT])

    solved = jnp.zeros_like(right)
    residual = right
    direction = right
    norm_now = jnp.sum(residual * residual, axis=-1, keepdims=True)
    for iteration in range(CG_ITERS):
        base = split_product(direction, gram_high, gram_low) + RIDGE * direction
        if iteration < CG_ITERS - 1:

            def scaled(i):
                scores = split_product(direction, high_t_ref[i], low_t_ref[i])
                return split(scores * weight_ref[i].astype(jnp.float32))

            def image_of(halves, i):
                both = dot(jnp.concatenate(halves, axis=0), high_ref[i])
                return both[:TILE] + both[TILE:] + dot(halves[0], low_ref[i])

            def apply(i, carry):
                running, high, low = carry
                running = running + image_of((high, low), i - 1)
                return (running,) + scaled(i)

            image, last_high, last_low = lax.fori_loop(1, chunks, apply, (base,) + scaled(0))
            image = image + image_of((last_high, last_low), chunks - 1)
            curve = jnp.sum(direction * image, axis=-1, keepdims=True)
        else:
            direction_halves = jnp.concatenate(split(direction), axis=0)

            def scores_of(i):
                both = dot(direction_halves, high_t_ref[i])
                return both[:TILE] + both[TILE:]

            def energy_of(scores, i):
                terms = scores * scores * weight_ref[i].astype(jnp.float32)
                parts = [terms[:, t * TILE:(t + 1) * TILE] for t in range(CHUNK)]
                return sum(parts[1:], parts[0])

            def energy(i, carry):
                running, scores = carry
                return running + energy_of(scores, i - 1), scores_of(i)

            initial = jnp.zeros((TILE, TILE), jnp.float32)
            energies, last_scores = lax.fori_loop(1, chunks, energy, (initial, scores_of(0)))
            energies = energies + energy_of(last_scores, chunks - 1)
            curve = jnp.sum(direction * base, axis=-1, keepdims=True) + jnp.sum(energies, axis=-1, keepdims=True)
        step = norm_now / curve
        solved = solved + step * direction
        if iteration < CG_ITERS - 1:
            residual = residual - step * image
            norm_next = jnp.sum(residual * residual, axis=-1, keepdims=True)
            direction = residual + norm_next / norm_now * direction
            norm_now = norm_next
    out_ref[...] = solved


def solve(first, count, places, gram, received, counts):
    smem = pl.BlockSpec(memory_space=pltpu.SMEM)
    vmem = pl.BlockSpec(memory_space=pltpu.VMEM)
    hbm = pl.BlockSpec(memory_space=pl.ANY)
    most = TILE // CHUNK
    return pl.pallas_call(
        functools.partial(solve_kernel, first, count),
        grid=(count,),
        out_shape=jax.ShapeDtypeStruct((count * TILE, FEAT), jnp.float32),
        in_specs=[smem, vmem] + [hbm] * 4,
        out_specs=pl.BlockSpec((TILE, FEAT), lambda b: (b, 0)),
        scratch_shapes=[
            pltpu.SMEM((count, TILE), jnp.int32),
            pltpu.SMEM((count,), jnp.int32),
            pltpu.VMEM((BUFFERS, CHUNK * TILE, FEAT), jnp.float32),
            pltpu.VMEM((BUFFERS, CHUNK, TILE, TILE), jnp.int32),
            pltpu.VMEM((most, CHUNK * TILE, FEAT), jnp.bfloat16),
            pltpu.VMEM((most, CHUNK * TILE, FEAT), jnp.bfloat16),
            pltpu.VMEM((most, FEAT, CHUNK * TILE), jnp.bfloat16),
            pltpu.VMEM((most, FEAT, CHUNK * TILE), jnp.bfloat16),
            pltpu.VMEM((most, TILE, CHUNK * TILE), jnp.bfloat16),
            pltpu.SemaphoreType.DMA((BUFFERS, 2)),
        ],
        cost_estimate=pl.CostEstimate(flops=8_000_000_000, bytes_accessed=16 << 20, transcendentals=0),
        compiler_params=pltpu.CompilerParams(vmem_limit_bytes=56 << 20),
        name=f"solve_{first}",
    )(places, gram, *received, counts)


def share_kernel(mine_ref, out_ref, send, recv, keep):
    me = my_coords()
    barrier = pltpu.get_barrier_semaphore()
    for offset in (1, 2, 3):
        pl.semaphore_signal(barrier, inc=1, device_id=device_at(shifted(me, "z", offset)), device_id_type=MESH)
    own = pltpu.make_async_copy(mine_ref, out_ref.at[me["z"]], keep)
    own.start()
    pl.semaphore_wait(barrier, 3)
    remotes = [
        pltpu.make_async_remote_copy(
            src_ref=mine_ref,
            dst_ref=out_ref.at[me["z"]],
            send_sem=send.at[offset],
            recv_sem=recv.at[offset],
            device_id=device_at(shifted(me, "z", offset)),
            device_id_type=MESH,
        )
        for offset in (1, 2, 3)
    ]
    for copy in remotes:
        copy.start()
    own.wait()
    for copy in remotes:
        copy.wait()


def share(mine):
    return pl.pallas_call(
        share_kernel,
        out_shape=jax.ShapeDtypeStruct((SIDE,) + mine.shape, jnp.float32),
        in_specs=[pl.BlockSpec(memory_space=pltpu.VMEM)],
        out_specs=pl.BlockSpec(memory_space=pltpu.VMEM),
        scratch_shapes=[
            pltpu.SemaphoreType.DMA((SIDE,)),
            pltpu.SemaphoreType.DMA((SIDE,)),
            pltpu.SemaphoreType.DMA,
        ],
        compiler_params=pltpu.CompilerParams(collective_id=2, has_side_effects=True),
        name="share",
    )(mine)


def body(item_factors, item_block, tile_user, tile_count, tile_counts):
    blocks_row = item_block[0]
    users_row = tile_user[0]
    live = jnp.arange(blocks_row.shape[0]) < tile_count[0]
    ids = jnp.stack([jnp.where(live, blocks_row, -1), jnp.where(live, users_row, UB_DEV)])
    ids = jnp.pad(ids, ((0, 6), (0, 0)))
    *received, gram, places = exchange(item_factors, ids, USUAL, 8, True, 0)
    again = gram[FEAT, 0] > 0
    _, received = lax.while_loop(
        lambda carry: carry[0],
        lambda carry: (jnp.zeros_like(again), tuple(exchange(item_factors, ids, MOST, 16, False, 1)[:PARTS])),
        (again, tuple(received)),
    )
    half = UB_DEV // 2
    earlier = solve(0, half, places, gram, received, tile_counts)
    earlier = lax.all_gather(earlier, "group", axis=0)
    later = solve(half, half, places, gram, received, tile_counts)
    return jnp.concatenate([earlier, share(later)], axis=1).reshape(-1, FEAT)


def solution(mesh):
    return jax.shard_map(
        body,
        mesh=mesh,
        in_specs=(
            P(("group", "shard"), None),
            P(("group", "shard"), None),
            P(("group", "shard"), None),
            P(("group", "shard")),
            P(("group", "shard"), None, None),
        ),
        out_specs=P("shard", None),
        check_vma=False,
    )
```
